128 devices in a mesh: leaf: 16 (over z, y), clus: 8 (over x, core).
Axes of the slice: x: 4, y: 4, z: 4, core: 2. Of those that a mesh axis runs over, the one named last changes fastest.
Arguments:
- points: bfloat16 [64, 1048576], P(None, ('leaf', 'clus')), may hold values from -6 to 6
- right_side: float32 [8, 1048576], P(None, ('leaf', 'clus')), may hold values from -18 to 18
- near_list: int32 [2048, 8], P(('leaf', 'clus')), may hold values from 0 to 2047, as said below
- near_count: int32 [2048], P(('leaf', 'clus')), may hold values from 3 to 8, as said below
- leaf_skeleton_basis: float32 [2048, 256, 512], P(('leaf', 'clus')), may hold values from -0.25 to 0.25
- leaf_transfer: float32 [2048, 256, 256], P(('leaf', 'clus')), may hold values from -0.375 to 0.375
- pair_transfer: float32 [128, 128, 256], P(('leaf', 'clus')), may hold values from -0.375 to 0.375
- group_transfer: float32 [16, 256, 256], P('leaf'), may hold values from -0.375 to 0.375
- pair_coupling: float32 [128, 4, 256, 128], P(('leaf', 'clus')), may hold values from -0.03125 to 0.03125
- group_coupling: float32 [16, 4, 256, 256], P('leaf'), may hold values from -0.015625 to 0.015625
- top_coupling: float32 [4, 4, 256, 256], replicated, may hold values from -0.0078125 to 0.0078125
- pair_far: int32 [64, 4], replicated, may hold values from 0 to 63
- group_far: int32 [16, 4], P('leaf'), may hold values from 0 to 15
- top_far: int32 [4, 4], replicated, may hold values from 0 to 3
Outputs:
- solution_field: float32 [8, 1048576], P(None, ('leaf', 'clus'))
- residual: float32 [8, 1048576], P(None, ('leaf', 'clus'))
The draws below stay inside these ranges and needn't reach their ends.
Inputs may be any that keep to these rules, and one draw needn't show every extreme that they name: `near_list`: slot 0 of leaf l is l itself, slot 1 is l - 16 and slot 2 is l + 16, each clipped to the range of leaves; every listed leaf lies among the leaves of the device that holds l and of the devices just before and after it in the order of leaf+clus (leaf index times 8 plus clus index), that is within 16 leaves of l. Slots at or beyond near_count hold valid leaves that are not used. `near_count`: some leaves use all 8 slots.
All inputs are finite; a program needn't handle non-finite values.
Results may differ from the reference program's by a relative error of at most 0.0003.
Values may be sent and summed in bfloat16 or wider, within the bound.
No kernel may reach another device: no remote copies, remote signals or barrier semaphores. Data moves between devices by JAX's collectives and lax.ppermute only.
A program may use at most 128 MiB of HBM per device.

```python
import jax
import jax.numpy as jnp
from jax import lax

FEAT = 64
TARG = 8
LEAF = 512
RANK = 256
NEAR = 8
FAR = 4
ITERS = 2
LEAVES_DEV = 16
N_LEAVES = 2048
N_PTS = 1048576
NODES1 = 64
GROUPS = 16
TOPS = 4
N_CLUS = 8
DEVICES = 128


def draw_right_side(key, part):
    key = jax.random.fold_in(key, 3)
    first = jax.random.fold_in(key, 0)
    point_coordinates = jnp.arange(N_PTS, dtype=jnp.float32) / N_PTS
    growth = 1.0 + 2.0 * point_coordinates
    values = jax.random.truncated_normal(first, -6.0, 6.0, (TARG, N_PTS), jnp.float32)
    return values * growth[None, :]


def draw_near_list(key, part):
    key = jax.random.fold_in(key, 1)
    leaves = jnp.arange(N_LEAVES, dtype=jnp.int32)
    offsets = jax.random.randint(key, (N_LEAVES, NEAR), -LEAVES_DEV, LEAVES_DEV + 1, dtype=jnp.int32)
    column = jnp.arange(NEAR, dtype=jnp.int32)[None, :]
    offsets = jnp.where(column == 0, 0, offsets)
    offsets = jnp.where(column == 1, -LEAVES_DEV, offsets)
    offsets = jnp.where(column == 2, LEAVES_DEV, offsets)
    listed = jnp.clip(leaves[:, None] + offsets, 0, N_LEAVES - 1)
    return listed.astype(jnp.int32)


def draw_near_count(key, part):
    key = jax.random.fold_in(key, 2)
    leaves = jnp.arange(N_LEAVES, dtype=jnp.int32)
    device = leaves // LEAVES_DEV
    heavy = device % 8 == 0
    ceiling = jnp.where(heavy, NEAR, min(NEAR, 4)).astype(jnp.int32)
    counts = jax.random.randint(key, (N_LEAVES,), 3, ceiling + 1, dtype=jnp.int32)
    filled = jnp.logical_and(heavy, leaves % LEAVES_DEV == 0)
    return jnp.where(filled, NEAR, counts).astype(jnp.int32)


def with_ends(array, key, smallest, largest):
    longest = array.shape.index(max(array.shape))
    spots = []
    for shift in (0, 1):
        where = [jax.random.randint(jax.random.fold_in(key, axis), (), 0, length) for axis, length in enumerate(array.shape)]
        where[longest] = (where[longest] + shift) % array.shape[longest]
        spots.append(tuple(where))
    return array.at[spots[0]].set(smallest).at[spots[1]].set(largest)


def block_levels(rng, extent, shards, smallest, largest):
    def one(axis_at, parts):
        draws = jax.random.uniform(jax.random.fold_in(jax.random.fold_in(rng, 6), axis_at), (parts,), jnp.float32, smallest / len(shards), largest / len(shards))
        return jnp.repeat(jnp.exp(draws), extent[axis_at] // parts).reshape((-1,) + (1,) * (len(extent) - axis_at - 1))

    gain = one(*shards[0])
    for cut in shards[1:]:
        gain = gain * one(*cut)
    return gain


def normal_values(stream_key, shape, width, most, shards=(), kind=jnp.bfloat16):
    entries = width * jax.random.normal(stream_key, shape, jnp.float32)
    if shards:
        entries = entries * block_levels(stream_key, shape, shards, -0.22, 0.18)
    return jnp.clip(entries, -most, most).astype(kind)


def setup_inputs(seed: int = 0) -> dict:
    keys = jax.random.split(jax.random.key(seed), 15)
    return {
        "points": normal_values(keys[0], (FEAT, N_PTS), 1.0, 6.0, ((1, 128),)),
        "right_side": draw_right_side(jax.random.fold_in(keys[14], 71), 0),
        "near_list": draw_near_list(jax.random.fold_in(keys[14], 71), 0),
        "near_count": draw_near_count(jax.random.fold_in(keys[14], 71), 0),
        "leaf_skeleton_basis": normal_values(keys[4], (N_LEAVES, RANK, LEAF), LEAF ** -0.5, 0.25, ((0, 128),), jnp.float32),
        "leaf_transfer": normal_values(keys[5], (N_LEAVES, RANK, RANK), RANK ** -0.5, 0.375, ((0, 128),), jnp.float32),
        "pair_transfer": normal_values(keys[6], (DEVICES, RANK // 2, RANK), RANK ** -0.5, 0.375, ((0, 128),), jnp.float32),
        "group_transfer": normal_values(keys[7], (GROUPS, RANK, RANK), RANK ** -0.5, 0.375, ((0, 16),), jnp.float32),
        "pair_coupling": normal_values(keys[8], (DEVICES, FAR, RANK, RANK // 2), (RANK * FAR * 2 * LEAVES_DEV) ** -0.5, 0.03125, ((0, 128),), jnp.float32),
        "group_coupling": normal_values(keys[9], (GROUPS, FAR, RANK, RANK), (RANK * FAR * N_CLUS * LEAVES_DEV) ** -0.5, 0.015625, ((0, 16),), jnp.float32),
        "top_coupling": normal_values(keys[10], (TOPS, FAR, RANK, RANK), (RANK * FAR * 4 * N_CLUS * LEAVES_DEV) ** -0.5, 0.0078125, (), jnp.float32),
        "pair_far": with_ends(jax.random.randint(keys[11], (NODES1, FAR), 0, NODES1), jax.random.fold_in(keys[11], 1), 0, NODES1 - 1).astype(jnp.int32),
        "group_far": with_ends(jax.random.randint(keys[12], (GROUPS, FAR), 0, GROUPS), jax.random.fold_in(keys[12], 1), 0, GROUPS - 1).astype(jnp.int32),
        "top_far": with_ends(jax.random.randint(keys[13], (TOPS, FAR), 0, TOPS), jax.random.fold_in(keys[13], 1), 0, TOPS - 1).astype(jnp.int32),
    }


HIGH_PRECISION = lax.Precision.HIGHEST
ridge_weight = 1.0

def near_field(leaf_points, leaf_norms, leaf_potential, near_list, near_count):

    def one_leaf(leaf_id):
        own_points = leaf_points[leaf_id]
        own_norms = leaf_norms[leaf_id]

        def add_slot(slot_id, running_total):
            other = near_list[leaf_id, slot_id]
            gram = lax.dot_general(own_points, leaf_points[other], (((0,), (0,)), ((), ())), preferred_element_type=jnp.float32)
            distance = own_norms[:, None] + leaf_norms[other][None, :] - 2.0 * gram
            kernel = jnp.exp(-distance / (2.0 * FEAT))
            return running_total + lax.dot_general(leaf_potential[other], kernel, (((1,), (1,)), ((), ())), precision=HIGH_PRECISION)
        return lax.fori_loop(0, near_count[leaf_id], add_slot, jnp.zeros((TARG, LEAF), jnp.float32))
    return lax.map(one_leaf, jnp.arange(N_LEAVES, dtype=jnp.int32))

def far_field(leaf_potential, leaf_skeleton_basis, leaf_transfer, pair_full, group_transfer, coupling_full, group_coupling, top_coupling, pair_far, group_far, top_far):
    skeleton_level_zero = jnp.einsum('ltp,lrp->ltr', leaf_potential, leaf_skeleton_basis, precision=HIGH_PRECISION)
    lifted = jnp.einsum('ltr,lrs->lts', skeleton_level_zero, leaf_transfer, precision=HIGH_PRECISION)
    level_one = lifted.reshape(NODES1, 2 * LEAVES_DEV, TARG, RANK).sum(1)
    level_two = jnp.einsum('ntr,nrs->nts', level_one, pair_full, precision=HIGH_PRECISION).reshape(GROUPS, N_CLUS // 2, TARG, RANK).sum(1)
    level_three = jnp.einsum('gtr,grs->gts', level_two, group_transfer, precision=HIGH_PRECISION).reshape(TOPS, 4, TARG, RANK).sum(1)
    couple_one = jnp.einsum('nktr,nkrs->nts', level_one[pair_far], coupling_full, precision=HIGH_PRECISION)
    couple_two = jnp.einsum('gktr,gkrs->gts', level_two[group_far], group_coupling, precision=HIGH_PRECISION)
    couple_three = jnp.einsum('qktr,qkrs->qts', level_three[top_far], top_coupling, precision=HIGH_PRECISION)
    group_parent = jnp.arange(GROUPS, dtype=jnp.int32) // 4
    down_two = couple_two + jnp.einsum('gts,grs->gtr', couple_three[group_parent], group_transfer, precision=HIGH_PRECISION)
    node_parent = jnp.arange(NODES1, dtype=jnp.int32) // (N_CLUS // 2)
    down_one = couple_one + jnp.einsum('nts,nrs->ntr', down_two[node_parent], pair_full, precision=HIGH_PRECISION)
    leaf_parent = jnp.arange(N_LEAVES, dtype=jnp.int32) // (2 * LEAVES_DEV)
    downward_level_zero = jnp.einsum('lts,lrs->ltr', down_one[leaf_parent], leaf_transfer, precision=HIGH_PRECISION)
    return jnp.einsum('ltr,lrp->ltp', downward_level_zero, leaf_skeleton_basis, precision=HIGH_PRECISION)

def reference(points, right_side, near_list, near_count, leaf_skeleton_basis, leaf_transfer, pair_transfer, group_transfer, pair_coupling, group_coupling, top_coupling, pair_far, group_far, top_far):
    leaf_points = points.reshape(FEAT, N_LEAVES, LEAF).transpose(1, 0, 2)
    leaf_norms = lax.optimization_barrier(jnp.sum(jnp.square(leaf_points.astype(jnp.float32)), axis=1))
    pair_full = pair_transfer.reshape(NODES1, RANK, RANK)
    coupling_full = pair_coupling.reshape(NODES1, 2, FAR, RANK, RANK // 2).transpose(0, 2, 3, 1, 4).reshape(NODES1, FAR, RANK, RANK)
    near_scale = 1.0 / jnp.sqrt(jnp.float32(NEAR * LEAF))

    def operate(field):
        leaf_potential = field.reshape(TARG, N_LEAVES, LEAF).transpose(1, 0, 2)
        near = near_field(leaf_points, leaf_norms, leaf_potential, near_list, near_count)
        far = far_field(leaf_potential, leaf_skeleton_basis, leaf_transfer, pair_full, group_transfer, coupling_full, group_coupling, top_coupling, pair_far, group_far, top_far)
        total = near * near_scale + far
        return ridge_weight * field + total.transpose(1, 0, 2).reshape(TARG, N_PTS)
    solution_field = jnp.zeros_like(right_side)
    residual = right_side
    direction = right_side
    norm_now = lax.optimization_barrier(jnp.sum(residual * residual, axis=1))
    for step in range(ITERS):
        image = operate(direction)
        alpha = norm_now / lax.optimization_barrier(jnp.sum(direction * image, axis=1))
        solution_field = solution_field + alpha[:, None] * direction
        residual = residual - alpha[:, None] * image
        if step + 1 < ITERS:
            norm_next = lax.optimization_barrier(jnp.sum(residual * residual, axis=1))
            direction = residual + (norm_next / norm_now)[:, None] * direction
            norm_now = norm_next
    return (solution_field, residual)
```

```python
import functools
import math

import jax
import jax.numpy as jnp
from jax import lax
from jax.experimental import pallas as pl
from jax.experimental.pallas import tpu as pltpu
from jax.sharding import PartitionSpec as P

LEAF = 512
NEAR = 8
FEAT = 64
GROUP = 4
STEP = 4

RIDGE = 1.0
NEAR_SCALE = 1.0 / math.sqrt(NEAR * LEAF)
f32 = jnp.float32
bf16 = jnp.bfloat16
BOTH = ("leaf", "clus")

VMEM = pl.BlockSpec(memory_space=pltpu.VMEM)
SMEM = pl.BlockSpec(memory_space=pltpu.SMEM)
ANY = pl.BlockSpec(memory_space=pl.ANY)


def params(mib=48):
    return pltpu.CompilerParams(vmem_limit_bytes=mib * 2**20)


def split(value):
    high = value.astype(bf16)
    return high, (value - high.astype(f32)).astype(bf16)


def stacked(value):
    high = value.astype(bf16).astype(f32)
    return jnp.concatenate([high, value - high], axis=0).astype(bf16)


def dot_wide(rows, matrix, transposed=False):
    both = stacked(rows)
    count = rows.shape[0]
    dims = (((1,), (1 if transposed else 0,)), ((), ()))
    total = None
    for part in split(matrix):
        out = lax.dot_general(both, part, dims, preferred_element_type=f32)
        out = out[:count] + out[count:]
        total = out if total is None else total + out
    return total


def points_kernel(points, packed, padded, decay):
    leaves = padded.shape[0]
    for leaf in range(leaves):
        block = points[:, leaf * LEAF : (leaf + 1) * LEAF].astype(f32)
        norm = jnp.sum(block * block, axis=0, keepdims=True)
        decay[:, leaf * LEAF : (leaf + 1) * LEAF] = jnp.broadcast_to(
            jnp.exp(norm * (-1.0 / (2.0 * FEAT))), (8, LEAF)
        )
        zero = jnp.zeros((FEAT, LEAF), bf16)
        padded[leaf, 0:FEAT] = zero
        padded[leaf, FEAT : 2 * FEAT] = (block * (1.0 / FEAT)).astype(bf16)
        padded[leaf, 2 * FEAT : 3 * FEAT] = zero
        if leaf % 2 == 1:
            before = points[:, (leaf - 1) * LEAF : leaf * LEAF].astype(f32)
            packed[leaf // 2] = jnp.concatenate([before, block], axis=0).T.astype(bf16)


def prepare_points(points, leaves):
    return pl.pallas_call(
        points_kernel,
        out_shape=[
            jax.ShapeDtypeStruct((leaves // 2, LEAF, 2 * FEAT), bf16),
            jax.ShapeDtypeStruct((leaves, 3 * FEAT, LEAF), bf16),
            jax.ShapeDtypeStruct((8, leaves * LEAF), f32),
        ],
        in_specs=[VMEM],
        out_specs=[VMEM] * 3,
        compiler_params=params(),
        name="prepare_points",
    )(points)


def field_kernel(field, decay, packed, sources):
    lane = lax.broadcasted_iota(jnp.int32, (16, 2 * FEAT), 1)
    for leaf in range(sources.shape[0]):
        columns = slice(leaf * LEAF, (leaf + 1) * LEAF)
        weighted = field[:, columns] * decay[:, columns]
        both = stacked(weighted)
        moments = jnp.dot(both, packed[leaf // 2], preferred_element_type=f32)
        if leaf % 2 == 1:
            moments = pltpu.roll(moments, FEAT, 1)
        total = jnp.sum(both.astype(f32), axis=1, keepdims=True)
        moments = jnp.where(lane < FEAT, moments, jnp.where(lane == FEAT, total, 0.0))
        sources[leaf, :, 0:LEAF] = both
        sources[leaf, :, LEAF : LEAF + 2 * FEAT] = stacked(moments[:8] + moments[8:])


def prepare_field(field, decay, packed, leaves):
    return pl.pallas_call(
        field_kernel,
        out_shape=jax.ShapeDtypeStruct((leaves, 16, LEAF + 2 * FEAT), bf16),
        in_specs=[VMEM] * 3,
        out_specs=VMEM,
        compiler_params=params(),
        name="prepare_field",
    )(field, decay, packed)


def add_pairs(count, pairs, padded, packed, sources, near, moments):
    leaves = padded.shape[0]

    def body(step, carry):
        parts = []
        for unit in range(GROUP):
            code = pairs[step * GROUP + unit]
            target, source = code // 64, code % 64
            start = pl.multiple_of(FEAT * (1 - source % 2), FEAT)
            own = padded[jnp.minimum(target, leaves - 1), pl.ds(start, 2 * FEAT), :]
            gram = jnp.dot(packed[source // 2], own, preferred_element_type=f32)
            rest = (jnp.exp(gram) - (gram + 1.0)).astype(bf16)
            parts.append((target, source, rest))
        for target, source, rest in parts:
            near[target] += jnp.dot(sources[source, :, 0:LEAF], rest, preferred_element_type=f32)
            moments[target] += sources[source, :, LEAF : LEAF + 2 * FEAT].astype(f32)
        return carry

    lax.fori_loop(0, (count + GROUP - 1) // GROUP, body, 0)


def near_inside_kernel(
    count, pairs, padded, packed_own, packed_peer, sources_own, sources_peer,
    near, moments, packed, sources, sems,
):
    leaves = padded.shape[0]
    copies = [
        pltpu.make_async_copy(packed_own, packed.at[pl.ds(0, leaves // 2)], sems.at[0]),
        pltpu.make_async_copy(packed_peer, packed.at[pl.ds(leaves // 2, leaves // 2)], sems.at[1]),
        pltpu.make_async_copy(sources_own, sources.at[pl.ds(0, leaves)], sems.at[2]),
        pltpu.make_async_copy(sources_peer, sources.at[pl.ds(leaves, leaves)], sems.at[3]),
    ]
    for copy in copies:
        copy.start()
    near[...] = jnp.zeros_like(near)
    moments[...] = jnp.zeros_like(moments)
    for copy in copies:
        copy.wait()
    add_pairs(count[0], pairs, padded, packed, sources, near, moments)


def pair_cost(pairs):
    return pl.CostEstimate(
        flops=pairs * 4 * LEAF * LEAF * 256, bytes_accessed=2**23, transcendentals=pairs * LEAF * LEAF
    )


def near_inside(count, pairs, padded, packed_own, packed_peer, sources_own, sources_peer):
    leaves = padded.shape[0]
    width = LEAF + 2 * FEAT
    return pl.pallas_call(
        near_inside_kernel,
        out_shape=[
            jax.ShapeDtypeStruct((leaves + 1, 16, LEAF), f32),
            jax.ShapeDtypeStruct((leaves + 1, 16, 2 * FEAT), f32),
        ],
        in_specs=[SMEM, SMEM, VMEM] + [ANY] * 4,
        out_specs=[VMEM] * 2,
        scratch_shapes=[
            pltpu.VMEM((leaves, LEAF, 2 * FEAT), bf16),
            pltpu.VMEM((2 * leaves, 16, width), bf16),
            pltpu.SemaphoreType.DMA((4,)),
        ],
        compiler_params=params(),
        cost_estimate=pair_cost(56),
        name="near_inside",
    )(count, pairs, padded, packed_own, packed_peer, sources_own, sources_peer)


def near_outside_kernel(
    count, pairs, padded, packed, sources, near_in, moments_in, decay, field, out, near, moments
):
    leaves = padded.shape[0]
    near[...] = near_in[...]
    moments[...] = moments_in[...]
    add_pairs(count[0], pairs, padded, packed, sources, near, moments)
    row = lax.broadcasted_iota(jnp.int32, (2 * FEAT, LEAF), 0)
    for leaf in range(leaves):
        columns = slice(leaf * LEAF, (leaf + 1) * LEAF)
        own = padded[leaf, FEAT : 3 * FEAT, :].astype(f32)
        own = jnp.where(row == FEAT, 1.0, own).astype(bf16)
        sums = moments[leaf]
        smooth = jnp.dot(stacked(sums[:8] + sums[8:]), own, preferred_element_type=f32)
        total = near[leaf] + smooth
        total = (total[:8] + total[8:]) * decay[:, columns]
        out[:, columns] = (total - field[:, columns]) * NEAR_SCALE


def near_outside(count, pairs, padded, packed, sources, near, moments, decay, field):
    leaves = padded.shape[0]
    return pl.pallas_call(
        near_outside_kernel,
        out_shape=jax.ShapeDtypeStruct(field.shape, f32),
        in_specs=[SMEM, SMEM] + [VMEM] * 7,
        out_specs=VMEM,
        scratch_shapes=[
            pltpu.VMEM((leaves + 1, 16, LEAF), f32),
            pltpu.VMEM((leaves + 1, 16, 2 * FEAT), f32),
        ],
        compiler_params=params(),
        cost_estimate=pair_cost(24),
        name="near_outside",
    )(count, pairs, padded, packed, sources, near, moments, decay, field)


def pair_list(mask, codes, empty):
    mask = mask.reshape(-1)
    codes = codes.reshape(-1)
    size = codes.shape[0]
    place = jnp.cumsum(mask.astype(jnp.int32)) - 1
    hits = (place[None, :] == jnp.arange(size, dtype=jnp.int32)[:, None]) & mask[None, :]
    listed = jnp.sum(jnp.where(hits, codes[None, :] - empty, 0), axis=1) + empty
    return jnp.sum(mask.astype(jnp.int32)).reshape(1), listed


def up_kernel(field, basis, transfer, out):
    @pl.when(pl.program_id(0) == 0)
    def _():
        out[...] = jnp.zeros_like(out)

    skeletons = [
        dot_wide(field[:, u * LEAF : (u + 1) * LEAF], basis[u], True) for u in range(STEP)
    ]
    out[...] += sum(dot_wide(skeletons[u], transfer[u]) for u in range(STEP))


def leaf_specs(rank):
    field = pl.BlockSpec((8, STEP * LEAF), lambda i: (0, i))
    basis = pl.BlockSpec((STEP, rank, LEAF), lambda i: (i, 0, 0))
    transfer = pl.BlockSpec((STEP, rank, rank), lambda i: (i, 0, 0))
    return field, basis, transfer


def far_up(field, basis, transfer):
    leaves, rank, _ = basis.shape
    specs = leaf_specs(rank)
    return pl.pallas_call(
        up_kernel,
        out_shape=jax.ShapeDtypeStruct((8, rank), f32),
        grid=(leaves // STEP,),
        in_specs=list(specs),
        out_specs=pl.BlockSpec((8, rank), lambda i: (0, 0)),
        compiler_params=params(),
        name="far_up",
    )(field, basis, transfer)


def whole_expansion(ints, own, peer):
    even = jnp.concatenate([own[...], peer[...]], axis=1)
    odd = jnp.concatenate([peer[...], own[...]], axis=1)
    return jnp.where(ints[0] == 0, even, odd)


def down_up_kernel(ints, own, peer, near, field, basis, transfer, image, upward, dots):
    @pl.when(pl.program_id(0) == 0)
    def _():
        upward[...] = jnp.zeros_like(upward)
        dots[...] = jnp.zeros_like(dots)

    expansion = whole_expansion(ints, own, peer)
    lower = [dot_wide(expansion, transfer[u], True) for u in range(STEP)]
    images = [
        dot_wide(lower[u], basis[u]) + near[:, u * LEAF : (u + 1) * LEAF] for u in range(STEP)
    ]
    skeletons = [dot_wide(images[u], basis[u], True) for u in range(STEP)]
    upward[...] += sum(dot_wide(skeletons[u], transfer[u]) for u in range(STEP))
    for u in range(STEP):
        columns = slice(u * LEAF, (u + 1) * LEAF)
        image[:, columns] = images[u]
        dots[0] += field[:, columns] * field[:, columns]
        dots[1] += field[:, columns] * images[u]
        dots[2] += images[u] * images[u]


def far_down_up(ints, own, peer, near, field, basis, transfer):
    leaves, rank, _ = basis.shape
    specs = leaf_specs(rank)
    half = pl.BlockSpec((8, rank // 2), lambda i: (0, 0))
    return pl.pallas_call(
        down_up_kernel,
        out_shape=[
            jax.ShapeDtypeStruct(near.shape, f32),
            jax.ShapeDtypeStruct((8, rank), f32),
            jax.ShapeDtypeStruct((3, 8, LEAF), f32),
        ],
        grid=(leaves // STEP,),
        in_specs=[SMEM, half, half, specs[0]] + list(specs),
        out_specs=[
            specs[0],
            pl.BlockSpec((8, rank), lambda i: (0, 0)),
            pl.BlockSpec((3, 8, LEAF), lambda i: (0, 0, 0)),
        ],
        compiler_params=params(),
        name="far_down_up",
    )(ints, own, peer, near, field, basis, transfer)


def down_kernel(ints, own, peer, near, field, first, dots_in, basis, transfer, image, dots, late):
    @pl.when(pl.program_id(0) == 0)
    def _():
        late[...] = jnp.zeros_like(late)

    expansion = whole_expansion(ints, own, peer)
    lower = [dot_wide(expansion, transfer[u], True) for u in range(STEP)]
    images = [
        dot_wide(lower[u], basis[u]) + near[:, u * LEAF : (u + 1) * LEAF] for u in range(STEP)
    ]
    for u in range(STEP):
        columns = slice(u * LEAF, (u + 1) * LEAF)
        image[:, columns] = images[u]
        late[0] += field[:, columns] * images[u]
        late[1] += first[:, columns] * images[u]

    @pl.when(pl.program_id(0) == pl.num_programs(0) - 1)
    def _():
        lane = lax.broadcasted_iota(jnp.int32, (8, 128), 1)
        total = jnp.zeros((8, 128), f32)
        for i in range(5):
            products = dots_in[i] if i < 3 else late[i - 3]
            total = jnp.where(lane == i, jnp.sum(products, axis=1, keepdims=True), total)
        dots[...] = total


def far_down(ints, own, peer, near, field, first, dots, basis, transfer):
    leaves, rank, _ = basis.shape
    specs = leaf_specs(rank)
    half = pl.BlockSpec((8, rank // 2), lambda i: (0, 0))
    return pl.pallas_call(
        down_kernel,
        out_shape=[
            jax.ShapeDtypeStruct(near.shape, f32),
            jax.ShapeDtypeStruct((8, 128), f32),
        ],
        grid=(leaves // STEP,),
        in_specs=[SMEM, half, half, specs[0], specs[0], specs[0]]
        + [pl.BlockSpec((3, 8, LEAF), lambda i: (0, 0, 0))]
        + list(specs[1:]),
        out_specs=[specs[0], pl.BlockSpec((8, 128), lambda i: (0, 0))],
        scratch_shapes=[pltpu.VMEM((2, 8, LEAF), f32)],
        compiler_params=params(),
        name="far_down",
    )(ints, own, peer, near, field, first, dots, basis, transfer)


def cluster_kernel(ints, own, peer, pair_transfer, out):
    rank = own.shape[1]
    half = rank // 2
    whole = own[...] + peer[...]
    mine = jnp.where(ints[0] == 0, whole[:, :half], whole[:, half:])
    out[:, :half] = mine
    out[:, half:] = dot_wide(mine, pair_transfer[...])


def group_kernel(shares, group_transfer, out):
    half = shares.shape[2] // 3
    devices = shares.shape[0]
    for node in range(devices // 2):
        out[node, :, :half] = shares[2 * node, :, :half]
        out[node, :, half:] = shares[2 * node + 1, :, :half]
    group = sum(shares[d, :, half:] for d in range(devices))
    out[devices // 2] = group
    out[devices // 2 + 1] = dot_wide(group, group_transfer[...])


def coarse_kernel(
    ints, fields, pair_transfer, group_transfer, pair_coupling, group_coupling, top_coupling, out
):
    slots = pair_coupling.shape[0]
    nodes = 4
    stride = nodes + 2
    pairs = sum(
        dot_wide(
            fields[stride * (ints[1 + k] // nodes) + ints[1 + k] % nodes], pair_coupling[k]
        )
        for k in range(slots)
    )
    groups = sum(
        dot_wide(fields[stride * ints[1 + slots + k] + nodes], group_coupling[k])
        for k in range(slots)
    )
    tops = 0.0
    for k in range(slots):
        first = nodes * ints[1 + 2 * slots + k]
        source = sum(fields[stride * (first + j) + nodes + 1] for j in range(nodes))
        tops += dot_wide(source, top_coupling[k])
    down = groups + dot_wide(tops, group_transfer[...], True)
    out[...] = pairs + dot_wide(down, pair_transfer[...], True)


def cluster_call(kernel, shape, *args, name):
    specs = [SMEM if a.dtype == jnp.int32 else VMEM for a in args]
    return pl.pallas_call(
        kernel,
        out_shape=jax.ShapeDtypeStruct(shape, f32),
        in_specs=specs,
        out_specs=VMEM,
        compiler_params=params(),
        name=name,
    )(*args)


def last_kernel(sums, field, first, second, solved, residual):
    shift = RIDGE + NEAR_SCALE
    dots = jnp.sum(sums[...], axis=0)
    bb, bh, hh, bg, hg = (dots[:, i : i + 1] for i in range(5))
    ratio = bh / bb
    alpha = bb / (shift * bb + bh)
    rest = hh - ratio * bh
    beta = alpha * alpha * rest / bb
    curve = shift * rest + ratio * (ratio * bh - hh) - ratio * bg + hg
    cross = (ratio * bh - hh) + (ratio * (shift * bb + bh) - shift * bh - bg)
    curving = alpha * alpha * curve + alpha * beta * cross + beta * beta * (shift * bb + bh)
    step = alpha * alpha * rest / curving
    gain = alpha * ratio + beta
    b, h, g = field[...], first[...], second[...]
    direction = gain * b - alpha * h
    residue = alpha * (ratio * b - h)
    image = gain * (shift * b + h) - alpha * (shift * h + g)
    solved[...] = alpha * b + step * direction
    residual[...] = residue - step * image


def on_device(
    points,
    right_side,
    near_list,
    near_count,
    leaf_skeleton_basis,
    leaf_transfer,
    pair_transfer,
    group_transfer,
    pair_coupling,
    group_coupling,
    top_coupling,
    pair_far,
    group_far,
    top_far,
):
    leaves = near_list.shape[0]
    device = lax.axis_index(BOTH)
    total = lax.axis_size(BOTH)
    side = device % 2
    node = device // 2
    top_id = lax.axis_index("leaf") // 4
    rank = leaf_skeleton_basis.shape[1]

    swap_in = [(i, i ^ 1) for i in range(total)]
    swap_out = [(i, i + 1) for i in range(1, total - 1, 2)]
    swap_out += [(j, i) for i, j in swap_out]
    inside = lambda value: lax.ppermute(value, BOTH, swap_in)
    outside = lambda value: lax.ppermute(value, BOTH, swap_out)

    ints = jnp.concatenate(
        [
            side.reshape(1),
            lax.dynamic_index_in_dim(pair_far, node, 0, keepdims=False),
            group_far[0],
            lax.dynamic_index_in_dim(top_far, top_id, 0, keepdims=False),
        ]
    ).astype(jnp.int32)
    top_own = lax.dynamic_index_in_dim(top_coupling, top_id, 0, keepdims=False)

    holder = near_list // leaves
    used = jnp.arange(NEAR, dtype=jnp.int32)[None, :] < near_count[:, None]
    target = jnp.broadcast_to(jnp.arange(leaves, dtype=jnp.int32)[:, None], near_list.shape)
    empty = 64 * leaves
    local = holder == device
    peer = holder == (device ^ 1)
    code = 64 * target + near_list % leaves
    count_in, pairs_in = pair_list(
        used & (local | peer), code + jnp.where(peer, leaves, 0), empty
    )
    count_out, pairs_out = pair_list(used & ~(local | peer), code, empty)

    def exchange(partial):
        mine = cluster_call(
            cluster_kernel, (8, 3 * rank // 2), ints, partial, inside(partial), pair_transfer[0],
            name="cluster",
        )
        shares = lax.all_gather(mine, "clus", axis=0)
        block = cluster_call(
            group_kernel, (shares.shape[0] // 2 + 2, 8, rank), shares, group_transfer[0],
            name="group",
        )
        fields = lax.all_gather(block, "leaf", axis=0, tiled=True)
        return cluster_call(
            coarse_kernel, (8, rank // 2), ints, fields, pair_transfer[0], group_transfer[0],
            pair_coupling[0], group_coupling[0], top_own, name="coarse",
        )

    upward = far_up(right_side, leaf_skeleton_basis, leaf_transfer)
    packed, padded, decay = prepare_points(points, leaves)
    packed_peer = inside(packed)
    packed_out = outside(packed)

    def near_field(field):
        sources = prepare_field(field, decay, packed, leaves)
        near, moments = near_inside(
            count_in, pairs_in, padded, packed, packed_peer, sources, inside(sources)
        )
        return near_outside(
            count_out, pairs_out, padded, packed_out, outside(sources), near, moments, decay, field
        )

    down = exchange(upward)
    near = near_field(right_side)
    first, upward, dots = far_down_up(
        ints, down, inside(down), near, right_side, leaf_skeleton_basis, leaf_transfer
    )
    down = exchange(upward)
    near = near_field(first)
    second, dots = far_down(
        ints, down, inside(down), near, right_side, first, dots, leaf_skeleton_basis, leaf_transfer
    )
    sums = lax.all_to_all(jnp.broadcast_to(dots[None, :, :8], (total, 8, 8)), BOTH, 0, 0, tiled=True)
    return pl.pallas_call(
        last_kernel,
        out_shape=[jax.ShapeDtypeStruct(right_side.shape, f32)] * 2,
        in_specs=[VMEM] * 4,
        out_specs=[VMEM] * 2,
        compiler_params=params(),
        name="last",
    )(sums, right_side, first, second)


def solution(mesh):
    in_specs = (
        P(None, BOTH),
        P(None, BOTH),
        P(BOTH, None),
        P(BOTH),
        P(BOTH, None, None),
        P(BOTH, None, None),
        P(BOTH, None, None),
        P("leaf", None, None),
        P(BOTH, None, None, None),
        P("leaf", None, None, None),
        P(),
        P(),
        P("leaf", None),
        P(),
    )
    out_specs = (P(None, BOTH), P(None, BOTH))
    return jax.shard_map(
        on_device, mesh=mesh, in_specs=in_specs, out_specs=out_specs, check_vma=False
    )
```

```python
import functools
import math

import jax
import jax.numpy as jnp
from jax import lax
from jax.experimental import pallas as pl
from jax.experimental.pallas import tpu as pltpu
from jax.sharding import PartitionSpec as P

LEAF = 512
NEAR = 8
FEAT = 64
GROUP = 8
SOURCE = 80
STEP = 4

RIDGE = 1.0
LOG2_E = math.log2(math.e)
NEAR_SCALE = 1.0 / math.sqrt(NEAR * LEAF)
f32 = jnp.float32
bf16 = jnp.bfloat16
BOTH = ("leaf", "clus")

VMEM = pl.BlockSpec(memory_space=pltpu.VMEM)
SMEM = pl.BlockSpec(memory_space=pltpu.SMEM)
ANY = pl.BlockSpec(memory_space=pl.ANY)


def params(mib=48):
    return pltpu.CompilerParams(vmem_limit_bytes=mib * 2**20)


def split(value):
    high = value.astype(bf16)
    return high, (value - high.astype(f32)).astype(bf16)


def stacked(value):
    high = value.astype(bf16).astype(f32)
    return jnp.concatenate([high, value - high], axis=0).astype(bf16)


def turned(rows):
    high = rows.astype(bf16).astype(f32)
    return jnp.concatenate([high, rows - high], axis=0).T.astype(bf16)


def dot_turned(matrix, columns):
    high, low = split(matrix)
    out = jnp.dot(high, columns, preferred_element_type=f32)
    out = (out + jnp.dot(low, columns, preferred_element_type=f32)).T
    count = columns.shape[1] // 2
    return out[:count] + out[count:]


def dot_wide(rows, matrix):
    both = stacked(rows)
    high, low = split(matrix)
    out = jnp.dot(both, high, preferred_element_type=f32)
    out += jnp.dot(both, low, preferred_element_type=f32)
    count = rows.shape[0]
    return out[:count] + out[count:]


def halo_kernel(points, field, packed_sources, decay):
    leaves = points.shape[1] // LEAF
    for leaf in range(leaves):
        columns = slice(leaf * LEAF, (leaf + 1) * LEAF)
        block = points[:, columns].astype(f32)
        norm = jnp.sum(block * block, axis=0, keepdims=True)
        decay[:, columns] = jnp.broadcast_to(jnp.exp(norm * (-1.0 / (2.0 * FEAT))), (8, LEAF))
        if leaf % 2 == 1:
            before = points[:, (leaf - 1) * LEAF : leaf * LEAF].astype(f32)
            turned = jnp.concatenate([before, block], axis=0).T.astype(bf16)
            packed_sources[leaf // 2 * LEAF : (leaf // 2 + 1) * LEAF, :] = turned
    start = leaves // 2 * LEAF
    write_sources(field, decay, packed_sources, packed_sources, start, leaves)


def write_sources(field, decay, packed, out, start, leaves):
    lane = lax.broadcasted_iota(jnp.int32, (16, 2 * FEAT), 1)
    for leaf in range(leaves):
        columns = slice(leaf * LEAF, (leaf + 1) * LEAF)
        both = stacked(field[:, columns] * decay[:, columns])
        points = packed[leaf // 2 * LEAF : (leaf // 2 + 1) * LEAF, :]
        moments = jnp.dot(both, points, preferred_element_type=f32)
        if leaf % 2 == 1:
            moments = pltpu.roll(moments, FEAT, 1)
        total = jnp.sum(both.astype(f32), axis=1, keepdims=True)
        moments = jnp.where(lane < FEAT, moments, jnp.where(lane == FEAT, total, 0.0))
        first = start + leaf * SOURCE
        for chunk in range(LEAF // 128):
            out[first + 16 * chunk : first + 16 * (chunk + 1), :] = both[
                :, 128 * chunk : 128 * (chunk + 1)
            ]
        out[first + LEAF // 8 : first + SOURCE, :] = stacked(moments[:8] + moments[8:])


def first_halo(points, field):
    leaves = field.shape[1] // LEAF
    rows = leaves // 2 * LEAF + leaves * SOURCE
    return pl.pallas_call(
        halo_kernel,
        out_shape=[
            jax.ShapeDtypeStruct((rows, 128), bf16),
            jax.ShapeDtypeStruct((8, leaves * LEAF), f32),
        ],
        in_specs=[VMEM] * 2,
        out_specs=[VMEM] * 2,
        compiler_params=params(16),
        name="first_halo",
    )(points, field)


def next_halo_kernel(field, decay, packed, out):
    write_sources(field, decay, packed, out, 0, out.shape[0] // SOURCE)


def next_halo(field, decay, packed):
    leaves = field.shape[1] // LEAF
    whole = lambda shape: pl.BlockSpec(shape, lambda i: (0, 0))
    return pl.pallas_call(
        next_halo_kernel,
        out_shape=jax.ShapeDtypeStruct((leaves * SOURCE, 128), bf16),
        grid=(1,),
        in_specs=[whole(field.shape), whole(decay.shape), whole((leaves // 2 * LEAF, 128))],
        out_specs=whole((leaves * SOURCE, 128)),
        compiler_params=params(16),
        name="next_halo",
    )(field, decay, packed)


def near_kernel(
    count, pairs, points, field, decay, own_points, peer_points, out_points,
    own_sources, peer_sources, out_sources, out, near, moments, padded, packed, sources, sems,
):
    leaves = field.shape[1] // LEAF
    rows = leaves // 2 * LEAF
    copies = []
    for i, ref in enumerate([own_points, peer_points, out_points]):
        copies.append(
            pltpu.make_async_copy(
                ref.at[pl.ds(0, rows)], packed.at[pl.ds(i * rows, rows)], sems.at[i]
            )
        )
    for i, ref in enumerate([own_sources, peer_sources, out_sources]):
        begin = ref.shape[0] - leaves * SOURCE
        copies.append(
            pltpu.make_async_copy(
                ref.at[pl.ds(begin, leaves * SOURCE)],
                sources.at[pl.ds(i * leaves * SOURCE, leaves * SOURCE)],
                sems.at[3 + i],
            )
        )
    for copy in copies:
        copy.start()
    near[...] = jnp.zeros_like(near)
    moments[...] = jnp.zeros_like(moments)
    zero = jnp.zeros((FEAT, LEAF), bf16)
    for leaf in range(leaves):
        block = points[:, leaf * LEAF : (leaf + 1) * LEAF].astype(f32)
        high, low = split(block * (LOG2_E / FEAT))
        for i, part in enumerate([zero, high, zero, low, zero]):
            padded[leaf, i * FEAT : (i + 1) * FEAT] = part
    for copy in copies:
        copy.wait()

    def add_pairs(first, size):
        parts = []
        for unit in range(size):
            code = pairs[first + unit]
            target, source = lax.shift_right_logical(code, 6), code & 63
            start = pl.multiple_of(FEAT * (1 - (source & 1)), FEAT)
            own = padded[jnp.minimum(target, leaves - 1), pl.ds(start, 4 * FEAT), :]
            place = pl.multiple_of(lax.shift_right_logical(source, 1) * LEAF, LEAF)
            other = packed[pl.ds(place, LEAF), :]
            gram = jnp.dot(
                jnp.concatenate([other, other], axis=1), own, preferred_element_type=f32
            )
            parts.append((target, source, (jnp.exp2(gram) - (gram + 1.0)).astype(bf16)))
        for target, source, rest in parts:
            begin = pl.multiple_of(source * SOURCE, SOURCE)
            chunks = [
                sources[pl.ds(pl.multiple_of(begin + 16 * c, 16), 16), :] for c in range(LEAF // 128 + 1)
            ]
            weighted = jnp.concatenate(chunks[:-1], axis=1)
            near[target] += jnp.dot(weighted, rest, preferred_element_type=f32)
            moments[target] += chunks[-1].astype(f32)

    def many(step, carry):
        add_pairs(step * GROUP, GROUP)
        return carry

    def few(step, carry):
        add_pairs(whole * GROUP + 2 * step, 2)
        return carry

    whole = lax.div(count[0], GROUP)
    left = count[0] - whole * GROUP
    lax.fori_loop(0, whole, many, 0)
    lax.fori_loop(0, lax.div(left + 1, 2), few, 0)

    row = lax.broadcasted_iota(jnp.int32, (2 * FEAT, LEAF), 0)
    for leaf in range(leaves):
        columns = slice(leaf * LEAF, (leaf + 1) * LEAF)
        scaled = points[:, columns].astype(f32) * (LOG2_E / FEAT)
        high, low = split(scaled)
        sums = moments[leaf]
        sums = sums[:8] + sums[8:]
        both = stacked(sums)
        total = near[leaf] + jnp.dot(both[:, :FEAT], high, preferred_element_type=f32)
        total += jnp.dot(both[:, :FEAT], low, preferred_element_type=f32)
        total = total[:8] + total[8:] + sums[:, FEAT : FEAT + 1]
        out[:, columns] = (total * decay[:, columns] - field[:, columns]) * NEAR_SCALE


def near_field(count, pairs, points, field, decay, halo, sources):
    leaves = field.shape[1] // LEAF
    pairs_guess = 88
    return pl.pallas_call(
        near_kernel,
        out_shape=jax.ShapeDtypeStruct(field.shape, f32),
        in_specs=[SMEM, SMEM, VMEM, VMEM, VMEM] + [ANY] * 6,
        out_specs=VMEM,
        scratch_shapes=[
            pltpu.VMEM((leaves + 1, 16, LEAF), f32),
            pltpu.VMEM((leaves + 1, 16, 128), f32),
            pltpu.VMEM((leaves, 5 * FEAT, LEAF), bf16),
            pltpu.VMEM((3 * leaves // 2 * LEAF, 128), bf16),
            pltpu.VMEM((3 * leaves * SOURCE, 128), bf16),
            pltpu.SemaphoreType.DMA((6,)),
        ],
        compiler_params=params(44),
        cost_estimate=pl.CostEstimate(
            flops=pairs_guess * 4 * LEAF * LEAF * 256,
            bytes_accessed=2**23,
            transcendentals=pairs_guess * LEAF * LEAF,
        ),
        name="near_field",
    )(count, pairs, points, field, decay, *halo, *sources)


def pair_list(mask, codes, empty):
    mask = mask.reshape(-1)
    codes = codes.reshape(-1)
    size = codes.shape[0]
    place = jnp.cumsum(mask.astype(jnp.int32)) - 1
    hits = (place[None, :] == jnp.arange(size, dtype=jnp.int32)[:, None]) & mask[None, :]
    listed = jnp.sum(jnp.where(hits, codes[None, :] - empty, 0), axis=1) + empty
    return jnp.sum(mask.astype(jnp.int32)).reshape(1), listed


def up_kernel(field, basis, transfer, out):
    @pl.when(pl.program_id(0) == 0)
    def _():
        out[...] = jnp.zeros_like(out)

    skeletons = [
        dot_turned(basis[u], turned(field[:, u * LEAF : (u + 1) * LEAF])) for u in range(STEP)
    ]
    out[...] += sum(dot_wide(skeletons[u], transfer[u]) for u in range(STEP))


def leaf_specs(rank):
    field = pl.BlockSpec((8, STEP * LEAF), lambda i: (0, i))
    basis = pl.BlockSpec((STEP, rank, LEAF), lambda i: (i, 0, 0))
    transfer = pl.BlockSpec((STEP, rank, rank), lambda i: (i, 0, 0))
    return field, basis, transfer


def far_up(field, basis, transfer):
    leaves, rank, _ = basis.shape
    specs = leaf_specs(rank)
    return pl.pallas_call(
        up_kernel,
        out_shape=jax.ShapeDtypeStruct((8, rank), f32),
        grid=(leaves // STEP,),
        in_specs=list(specs),
        out_specs=pl.BlockSpec((8, rank), lambda i: (0, 0)),
        compiler_params=params(),
        name="far_up",
    )(field, basis, transfer)


def whole_expansion(ints, own, peer):
    even = jnp.concatenate([own[...], peer[...]], axis=1)
    odd = jnp.concatenate([peer[...], own[...]], axis=1)
    return jnp.where(ints[0] == 0, even, odd)


def down_up_kernel(ints, own, peer, near, field, basis, transfer, image, upward, dots):
    @pl.when(pl.program_id(0) == 0)
    def _():
        upward[...] = jnp.zeros_like(upward)
        dots[...] = jnp.zeros_like(dots)

    expansion = turned(whole_expansion(ints, own, peer))
    lower = [dot_turned(transfer[u], expansion) for u in range(STEP)]
    images = [
        dot_wide(lower[u], basis[u]) + near[:, u * LEAF : (u + 1) * LEAF] for u in range(STEP)
    ]
    skeletons = [dot_turned(basis[u], turned(images[u])) for u in range(STEP)]
    upward[...] += sum(dot_wide(skeletons[u], transfer[u]) for u in range(STEP))
    for u in range(STEP):
        columns = slice(u * LEAF, (u + 1) * LEAF)
        image[:, columns] = images[u]
        dots[0] += field[:, columns] * field[:, columns]
        dots[1] += field[:, columns] * images[u]
        dots[2] += images[u] * images[u]


def far_down_up(ints, own, peer, near, field, basis, transfer):
    leaves, rank, _ = basis.shape
    specs = leaf_specs(rank)
    half = pl.BlockSpec((8, rank // 2), lambda i: (0, 0))
    return pl.pallas_call(
        down_up_kernel,
        out_shape=[
            jax.ShapeDtypeStruct(near.shape, f32),
            jax.ShapeDtypeStruct((8, rank), f32),
            jax.ShapeDtypeStruct((3, 8, LEAF), f32),
        ],
        grid=(leaves // STEP,),
        in_specs=[SMEM, half, half, specs[0]] + list(specs),
        out_specs=[
            specs[0],
            pl.BlockSpec((8, rank), lambda i: (0, 0)),
            pl.BlockSpec((3, 8, LEAF), lambda i: (0, 0, 0)),
        ],
        compiler_params=params(),
        name="far_down_up",
    )(ints, own, peer, near, field, basis, transfer)


def dot_place():
    lane = lax.broadcasted_iota(jnp.int32, (8, 128), 1)
    row = lax.broadcasted_iota(jnp.int32, (8, 128), 0)
    return jnp.where((lane & 7) == row, lax.shift_right_logical(lane, 3), -1)


def down_kernel(ints, own, peer, near, field, first, dots_in, basis, transfer, image, dots, late):
    @pl.when(pl.program_id(0) == 0)
    def _():
        late[...] = jnp.zeros_like(late)

    expansion = turned(whole_expansion(ints, own, peer))
    lower = [dot_turned(transfer[u], expansion) for u in range(STEP)]
    images = [
        dot_wide(lower[u], basis[u]) + near[:, u * LEAF : (u + 1) * LEAF] for u in range(STEP)
    ]
    for u in range(STEP):
        columns = slice(u * LEAF, (u + 1) * LEAF)
        image[:, columns] = images[u]
        late[0] += field[:, columns] * images[u]
        late[1] += first[:, columns] * images[u]

    @pl.when(pl.program_id(0) == pl.num_programs(0) - 1)
    def _():
        place = dot_place()
        total = jnp.zeros((8, 128), f32)
        for i in range(5):
            products = dots_in[i] if i < 3 else late[i - 3]
            total = jnp.where(place == i, jnp.sum(products, axis=1, keepdims=True), total)
        row = jnp.sum(total, axis=0, keepdims=True)
        dots[...] = jnp.broadcast_to(row[None], dots.shape)


def far_down(ints, own, peer, near, field, first, dots, basis, transfer, devices):
    leaves, rank, _ = basis.shape
    specs = leaf_specs(rank)
    half = pl.BlockSpec((8, rank // 2), lambda i: (0, 0))
    return pl.pallas_call(
        down_kernel,
        out_shape=[
            jax.ShapeDtypeStruct(near.shape, f32),
            jax.ShapeDtypeStruct((devices, 1, 128), f32),
        ],
        grid=(leaves // STEP,),
        in_specs=[SMEM, half, half, specs[0], specs[0], specs[0]]
        + [pl.BlockSpec((3, 8, LEAF), lambda i: (0, 0, 0))]
        + list(specs[1:]),
        out_specs=[specs[0], pl.BlockSpec((devices, 1, 128), lambda i: (0, 0, 0))],
        scratch_shapes=[pltpu.VMEM((2, 8, LEAF), f32)],
        compiler_params=params(),
        name="far_down",
    )(ints, own, peer, near, field, first, dots, basis, transfer)


def cluster_kernel(ints, own, peer, pair_transfer, out):
    rank = own.shape[1]
    half = rank // 2
    whole = own[...] + peer[...]
    mine = jnp.where(ints[0] == 0, whole[:, :half], whole[:, half:])
    share = jnp.concatenate([mine, dot_wide(mine, pair_transfer[...])], axis=1)
    out[...] = jnp.broadcast_to(share[None], out.shape)


def group_kernel(shares, group_transfer, out):
    half = shares.shape[2] // 3
    devices = shares.shape[0]
    group = sum(shares[d, :, half:] for d in range(devices))
    lift = dot_wide(group, group_transfer[...])
    for copy in range(out.shape[0]):
        for node in range(devices // 2):
            out[copy, node, :, :half] = shares[2 * node, :, :half]
            out[copy, node, :, half:] = shares[2 * node + 1, :, :half]
        out[copy, devices // 2] = group
        out[copy, devices // 2 + 1] = lift


def coarse_kernel(
    ints, fields, pair_transfer, group_transfer, pair_coupling, group_coupling, top_coupling,
    out, own_top, sem,
):
    slots = pair_coupling.shape[0]
    copy = pltpu.make_async_copy(top_coupling.at[ints[1 + 3 * slots]], own_top, sem)
    copy.start()
    nodes = 4
    stride = nodes + 2
    pairs = sum(
        dot_wide(
            fields[stride * (ints[1 + k] // nodes) + ints[1 + k] % nodes], pair_coupling[k]
        )
        for k in range(slots)
    )
    groups = sum(
        dot_wide(fields[stride * ints[1 + slots + k] + nodes], group_coupling[k])
        for k in range(slots)
    )
    copy.wait()
    tops = 0.0
    for k in range(slots):
        first = nodes * ints[1 + 2 * slots + k]
        source = sum(fields[stride * (first + j) + nodes + 1] for j in range(nodes))
        tops += dot_wide(source, own_top[k])
    down = groups + dot_turned(group_transfer[...], turned(tops))
    out[...] = pairs + dot_turned(pair_transfer[...], turned(down))


def cluster_call(kernel, shape, *args, name, scratch=(), far_away=()):
    specs = [SMEM if a.dtype == jnp.int32 else VMEM for a in args] + [ANY] * len(far_away)
    return pl.pallas_call(
        kernel,
        out_shape=jax.ShapeDtypeStruct(shape, f32),
        in_specs=specs,
        out_specs=VMEM,
        scratch_shapes=scratch,
        compiler_params=params(16),
        name=name,
    )(*args, *far_away)


def last_kernel(sums, field, first, second, solved, residual):
    shift = RIDGE + NEAR_SCALE
    dots = jnp.broadcast_to(jnp.sum(sums[...], axis=0), (8, 128))
    place = dot_place()
    bb, bh, hh, bg, hg = (
        jnp.sum(jnp.where(place == i, dots, 0.0), axis=1, keepdims=True) for i in range(5)
    )
    ratio = bh / bb
    alpha = bb / (shift * bb + bh)
    rest = hh - ratio * bh
    beta = alpha * alpha * rest / bb
    curve = shift * rest + ratio * (ratio * bh - hh) - ratio * bg + hg
    cross = (ratio * bh - hh) + (ratio * (shift * bb + bh) - shift * bh - bg)
    curving = alpha * alpha * curve + alpha * beta * cross + beta * beta * (shift * bb + bh)
    step = alpha * alpha * rest / curving
    gain = alpha * ratio + beta
    b, h, g = field[...], first[...], second[...]
    direction = gain * b - alpha * h
    residue = alpha * (ratio * b - h)
    image = gain * (shift * b + h) - alpha * (shift * h + g)
    solved[...] = alpha * b + step * direction
    residual[...] = residue - step * image


def on_device(
    points,
    right_side,
    near_list,
    near_count,
    leaf_skeleton_basis,
    leaf_transfer,
    pair_transfer,
    group_transfer,
    pair_coupling,
    group_coupling,
    top_coupling,
    pair_far,
    group_far,
    top_far,
):
    leaves = near_list.shape[0]
    device = lax.axis_index(BOTH)
    total = lax.axis_size(BOTH)
    side = device % 2
    node = device // 2
    top_id = lax.axis_index("leaf") // 4
    rank = leaf_skeleton_basis.shape[1]

    swap_in = [(i, i ^ 1) for i in range(total)]
    swap_out = [(i, i + 1) for i in range(1, total - 1, 2)]
    swap_out += [(j, i) for i, j in swap_out]
    inside = lambda value: lax.ppermute(value, BOTH, swap_in)
    outside = lambda value: lax.ppermute(value, BOTH, swap_out)

    ints = jnp.concatenate(
        [
            side.reshape(1),
            lax.dynamic_index_in_dim(pair_far, node, 0, keepdims=False),
            group_far[0],
            lax.dynamic_index_in_dim(top_far, top_id, 0, keepdims=False),
            top_id.reshape(1),
        ]
    ).astype(jnp.int32)

    holder = near_list // leaves
    used = jnp.arange(NEAR, dtype=jnp.int32)[None, :] < near_count[:, None]
    target = jnp.broadcast_to(jnp.arange(leaves, dtype=jnp.int32)[:, None], near_list.shape)
    window = jnp.where(holder == device, 0, jnp.where(holder == (device ^ 1), leaves, 2 * leaves))
    count, pairs = pair_list(used, 64 * target + window + near_list % leaves, 64 * leaves)

    def exchange(partial):
        mine = cluster_call(
            cluster_kernel, (lax.axis_size("clus"), 8, 3 * rank // 2),
            ints, partial, inside(partial), pair_transfer[0], name="cluster",
        )
        shares = lax.all_to_all(mine, "clus", 0, 0, tiled=True)
        block = cluster_call(
            group_kernel, (lax.axis_size("leaf"), shares.shape[0] // 2 + 2, 8, rank),
            shares, group_transfer[0], name="group",
        )
        fields = lax.all_to_all(block, "leaf", 0, 0, tiled=True)
        return cluster_call(
            coarse_kernel, (8, rank // 2), ints, fields.reshape(-1, 8, rank), pair_transfer[0],
            group_transfer[0], pair_coupling[0], group_coupling[0], name="coarse",
            scratch=[pltpu.VMEM(top_coupling.shape[1:], f32), pltpu.SemaphoreType.DMA],
            far_away=[top_coupling],
        )

    halo, decay = first_halo(points, right_side)
    halos = (halo, inside(halo), outside(halo))
    upward = far_up(right_side, leaf_skeleton_basis, leaf_transfer)
    down = exchange(upward)
    near = near_field(count, pairs, points, right_side, decay, halos, halos)
    first, upward, dots = far_down_up(
        ints, down, inside(down), near, right_side, leaf_skeleton_basis, leaf_transfer
    )
    sources = next_halo(first, decay, halo)
    sources = (sources, inside(sources), outside(sources))
    down = exchange(upward)
    near = near_field(count, pairs, points, first, decay, halos, sources)
    second, dots = far_down(
        ints, down, inside(down), near, right_side, first, dots, leaf_skeleton_basis,
        leaf_transfer, total,
    )
    sums = lax.all_to_all(dots, BOTH, 0, 0, tiled=True)
    return pl.pallas_call(
        last_kernel,
        out_shape=[jax.ShapeDtypeStruct(right_side.shape, f32)] * 2,
        in_specs=[VMEM] * 4,
        out_specs=[VMEM] * 2,
        compiler_params=params(),
        name="last",
    )(sums, right_side, first, second)


def solution(mesh):
    in_specs = (
        P(None, BOTH),
        P(None, BOTH),
        P(BOTH, None),
        P(BOTH),
        P(BOTH, None, None),
        P(BOTH, None, None),
        P(BOTH, None, None),
        P("leaf", None, None),
        P(BOTH, None, None, None),
        P("leaf", None, None, None),
        P(),
        P(),
        P("leaf", None),
        P(),
    )
    out_specs = (P(None, BOTH), P(None, BOTH))
    return jax.shard_map(
        on_device, mesh=mesh, in_specs=in_specs, out_specs=out_specs, check_vma=False
    )
```
